32 devices in a mesh: group: 2 (over y), cell: 8 (over z, x), head: 2 (over core).
Axes of the slice: x: 2, y: 2, z: 4, core: 2. Of those that a mesh axis runs over, the one named last changes fastest.
Arguments:
- latents: bfloat16 [4096, 1024], P(('group', 'cell')), parts along dimension 0, may hold values from -6.2 to 6.2
- cells: bfloat16 [16384, 1024], P(('group', 'cell')), parts along dimension 0, may hold values from -6 to 6
- w_query: bfloat16 [1024, 1024], P(None, 'head'), may hold values from -1.53125 to 1.53125
- w_key: bfloat16 [1024, 1024], P(None, 'head'), may hold values from -0.134375 to 0.134375
- w_value: bfloat16 [1024, 1024], P(None, 'head'), may hold values from -0.1875 to 0.1875
- w_out: bfloat16 [1024, 1024], replicated, may hold values from -0.1875 to 0.1875
- w_up: bfloat16 [1024, 4096], P(None, ('cell', 'head')), may hold values from -0.1875 to 0.1875
- w_down: bfloat16 [4096, 1024], P(('cell', 'head')), may hold values from -0.09375 to 0.09375
Outputs:
- prototypes: bfloat16 [4096, 1024], P(('group', 'cell', 'head')), parts along dimension 0
The draws below stay inside these ranges and needn't reach their ends.
There are 2 independent parts, one for each index of `group`. The reference program is written for one: setup_inputs(seed, part) draws one part's arguments, and reference() takes and returns one part's arrays. A program takes and returns all parts, laid end to end along the dimension named above; an argument that names none is the same for every part. Nothing has to cross between parts.
All inputs are finite; a program needn't handle non-finite values.
Results may differ from the reference program's by a relative error of at most 0.015.
Values may be sent and summed in bfloat16 or wider, within the bound.
A program may use at most 128 MiB of HBM per device.

```python
import jax
import jax.numpy as jnp
from jax import lax

D = 1024
HEADS = 16
HEAD_DIM = 64
LAT = 2048
FF = 4096
CELL_DEV = 1024
CELLS = 8192
N_CELL = 8


def draw_cells(key, part):
    return jnp.clip(jax.random.normal(jax.random.fold_in(key, 205), (CELLS, D), jnp.float32), -6.0, 6.0).astype(jnp.bfloat16)


def draw_latents(key, part):
    return jnp.clip(jax.random.normal(jax.random.fold_in(key, 207), (LAT, D), jnp.float32), -6.0, 6.0).astype(jnp.bfloat16)


def draw_w_query(key, part):
    return (3.0 * D ** (-0.5) * jnp.clip(jax.random.normal(jax.random.fold_in(key, 302), (D, D), jnp.float32), -4.0, 4.0)).astype(jnp.bfloat16)


def draw_w_key(key, part):
    return (D ** (-0.5) * jnp.clip(jax.random.normal(jax.random.fold_in(key, 304), (D, D), jnp.float32), -4.0, 4.0)).astype(jnp.bfloat16)


def block_levels(stream_key, shape, shards, smallest, high):
    def one(position, blocks):
        heights = jax.random.uniform(jax.random.fold_in(jax.random.fold_in(stream_key, 6), position), (blocks,), jnp.float32, smallest / len(shards), high / len(shards))
        return jnp.repeat(jnp.exp(heights), shape[position] // blocks).reshape((-1,) + (1,) * (len(shape) - position - 1))

    gain = one(*shards[0])
    for cut in shards[1:]:
        gain = gain * one(*cut)
    return gain


def normal_values(rng, extent, deviation, bound, cuts=(), kind=jnp.bfloat16):
    array = jax.random.normal(rng, extent, jnp.float32) * deviation
    if len(cuts) > 0:
        array = block_levels(rng, extent, cuts, -0.22, 0.18) * array
    return jnp.clip(array, min=-bound, max=bound).astype(kind)


def setup_inputs(seed: int = 0, part: int = 0) -> dict:
    splits = jax.random.split(jax.random.key(seed), 9)
    own_keys = jax.random.split(jax.random.fold_in(splits[8], part), 9)
    latents = draw_latents(jax.random.fold_in(jax.random.fold_in(splits[8], part), 71), part)
    cells = draw_cells(jax.random.fold_in(jax.random.fold_in(splits[8], part), 71), part)
    w_query = draw_w_query(jax.random.fold_in(splits[8], 71), part)
    w_key = draw_w_key(jax.random.fold_in(splits[8], 71), part)
    w_value = normal_values(splits[4], (D, D), D ** -0.5, 0.1875, ((1, 2),))
    w_out = normal_values(splits[5], (D, D), D ** -0.5, 0.1875)
    w_up = normal_values(splits[6], (D, FF), D ** -0.5, 0.1875, ((1, 16),))
    w_down = normal_values(splits[7], (FF, D), FF ** -0.5, 0.09375, ((0, 16),))
    return {"latents": latents, "cells": cells, "w_query": w_query, "w_key": w_key, "w_value": w_value, "w_out": w_out, "w_up": w_up, "w_down": w_down}


def reference(latents, cells, w_query, w_key, w_value, w_out, w_up, w_down):
    queries = jnp.dot(latents, w_query, preferred_element_type=jnp.float32).astype(jnp.bfloat16)
    key_rows = jnp.dot(cells, w_key, preferred_element_type=jnp.float32).astype(jnp.bfloat16)
    value_rows = jnp.dot(cells, w_value, preferred_element_type=jnp.float32).astype(jnp.bfloat16)
    factor = HEAD_DIM ** (-0.5)
    query_heads = jnp.transpose(queries.reshape(LAT, HEADS, HEAD_DIM), (1, 0, 2)).astype(jnp.float32)

    def one_block(carry, block_index):
        old_max, old_tot, old_sum = carry
        start = (block_index * CELL_DEV).astype(jnp.int32)
        key_block = lax.dynamic_slice_in_dim(key_rows, start, CELL_DEV, 0).reshape(CELL_DEV, HEADS, HEAD_DIM).astype(jnp.float32)
        value_block = lax.dynamic_slice_in_dim(value_rows, start, CELL_DEV, 0).reshape(CELL_DEV, HEADS, HEAD_DIM).astype(jnp.float32)
        scores = jnp.einsum('hld,chd->hlc', query_heads, key_block) * factor
        block_max = lax.optimization_barrier(jnp.max(scores, axis=2))
        weights = jnp.exp(scores - block_max[:, :, None])
        block_tot = lax.optimization_barrier(jnp.sum(weights, axis=2))
        rounded = lax.optimization_barrier(weights.astype(jnp.bfloat16))
        block_sum = jnp.einsum('hlc,chd->hld', rounded.astype(jnp.float32), value_block)
        new_max = jnp.maximum(old_max, block_max)
        keep = jnp.exp(old_max - new_max)
        fresh = jnp.exp(block_max - new_max)
        new_tot = old_tot * keep + block_tot * fresh
        new_sum = old_sum * keep[:, :, None] + block_sum * fresh[:, :, None]
        return ((new_max, new_tot, new_sum), None)
    start_carry = (jnp.full((HEADS, LAT), -1e+30, jnp.float32), jnp.zeros((HEADS, LAT), jnp.float32), jnp.zeros((HEADS, LAT, HEAD_DIM), jnp.float32))
    final, unused = lax.scan(one_block, start_carry, jnp.arange(N_CELL, dtype=jnp.int32))
    maxima, totals, summed = final
    attended = (summed / totals[:, :, None]).astype(jnp.bfloat16)
    attended = jnp.transpose(attended, (1, 0, 2)).reshape(LAT, D)
    updated = (latents.astype(jnp.float32) + jnp.dot(attended, w_out, preferred_element_type=jnp.float32)).astype(jnp.bfloat16)
    widened = updated.astype(jnp.float32)
    normed = (widened * lax.rsqrt(lax.optimization_barrier(jnp.mean(widened * widened, axis=1, keepdims=True)) + 1e-05)).astype(jnp.bfloat16)
    hidden = jax.nn.gelu(jnp.dot(normed, w_up, preferred_element_type=jnp.float32), approximate=True).astype(jnp.bfloat16)
    return (widened + jnp.dot(hidden, w_down, preferred_element_type=jnp.float32)).astype(jnp.bfloat16)
```

```python
import functools
import math

import jax
import jax.numpy as jnp
from jax import lax
from jax.experimental import pallas as pl
from jax.experimental.pallas import tpu as pltpu
from jax.sharding import PartitionSpec as P

HEAD_DIM = 64
PAIR = 2 * HEAD_DIM
EXTRA = 16
F32 = jnp.float32
BF16 = jnp.bfloat16
SCALE = HEAD_DIM ** (-0.5) * math.log2(math.e)


def dot(a, b):
    return jnp.dot(a, b, preferred_element_type=F32)


def kernel(
    n,
    lat_ref, cells_ref, wq_ref, wk_ref, wv_ref, wo_ref, wu_ref, wd_ref, out_ref,
    q, kz, vt, wus, wds,
    own, part, xin, zin, own_s, part_s, xin_s, zin_s,
    acc, att, att_in, upd, nrm, mown, mpart, mxin, mzin, macc,
    w_sem, q_zs, q_xs, q_r,
    p_zs, p_zr, p_xs, p_xr,
    ps_zs, ps_zr, ps_xs, ps_xr,
    a_sem, n_zs, n_xs, n_r, m_zs, m_zr, m_xs, m_xr,
):
    na = n // 2
    me = lax.axis_index("cell")
    head = lax.axis_index("head")
    a, b = me // 2, me % 2
    across = a * 2 + 1 - b
    heads = wq_ref.shape[1] // HEAD_DIM
    width = wq_ref.shape[1]
    half = out_ref.shape[0]
    count = cells_ref.shape[0]

    def peer(d):
        return (a + d) % na

    def send(src, dst, ss, rs, **where):
        return pltpu.make_async_remote_copy(
            src_ref=src, dst_ref=dst, send_sem=ss, recv_sem=rs,
            device_id=where, device_id_type=pl.DeviceIdType.MESH,
        )

    def each(low, high, f):
        def step(i, carry):
            f(i)
            return carry
        lax.fori_loop(low, high, step, 0)

    barrier = pltpu.get_barrier_semaphore()
    each(1, na, lambda d: pl.semaphore_signal(
        barrier, inc=1, device_id={"cell": peer(d) * 2 + b},
        device_id_type=pl.DeviceIdType.MESH))
    pl.semaphore_signal(barrier, inc=1, device_id={"cell": across},
                        device_id_type=pl.DeviceIdType.MESH)
    pl.semaphore_signal(barrier, inc=1, device_id={"head": 1 - head},
                        device_id_type=pl.DeviceIdType.MESH)
    q[me] = dot(lat_ref[...], wq_ref[...]).astype(BF16)
    pl.semaphore_wait(barrier, na + 1)

    def to_z(buf, zs, r, d):
        return send(buf.at[me], buf.at[me], zs.at[d], r.at[me], cell=peer(d) * 2 + b)

    def to_x(buf, xs, r, ap):
        slot = ap * 2 + b
        return send(buf.at[slot], buf.at[slot], xs.at[ap], r.at[slot], cell=across)

    def arrived(buf, xs, r, slot):
        send(buf.at[slot], buf.at[slot], xs.at[0], r.at[slot], cell=across).wait_recv()

    def gather_start(buf, zs, xs, r):
        to_x(buf, xs, r, a).start()
        each(1, na, lambda d: to_z(buf, zs, r, d).start())

    def forward(buf, xs, r, d):
        ap = peer(d)
        arrived(buf, xs, r, ap * 2 + b)
        to_x(buf, xs, r, ap).start()

    def gather_finish(buf, zs, xs, r):
        each(1, na, lambda d: to_z(buf, zs, r, d).wait_send())
        each(0, na, lambda ap: to_x(buf, xs, r, ap).wait_send())

    gather_start(q, q_zs, q_xs, q_r)
    up_copy = send(wu_ref, wus, w_sem.at[0], w_sem.at[1], head=1 - head)
    down_copy = send(wd_ref, wds, w_sem.at[2], w_sem.at[3], head=1 - head)
    up_copy.start()
    down_copy.start()

    tile = 256

    def project(t):
        rows = pl.ds(pl.multiple_of(t * tile, tile), tile)
        block = cells_ref[rows, :]
        k = dot(block, wk_ref[...]).astype(BF16)
        v = dot(block, wv_ref[...]).T.astype(BF16)
        lane = lax.broadcasted_iota(jnp.int32, (tile, PAIR), 1)
        for h in range(heads):
            pair = k[:, (h // 2) * PAIR:(h // 2 + 1) * PAIR]
            keep = (lane < HEAD_DIM) if h % 2 == 0 else (lane >= HEAD_DIM)
            kz[h, rows, :] = jnp.where(keep, pair, jnp.zeros_like(pair))
            vt[h, :HEAD_DIM, rows] = v[h * HEAD_DIM:(h + 1) * HEAD_DIM, :]
            vt[h, HEAD_DIM:, rows] = jnp.ones((EXTRA, tile), BF16)

    each(0, count // tile, project)

    def attend(slot, oref, sref, k):
        def pair_step(p):
            q2 = q[slot, :, pl.ds(pl.multiple_of(p * PAIR, PAIR), PAIR)]
            for e in range(2):
                h = 2 * p + e
                s = lax.dot_general(kz[h], q2, (((1,), (1,)), ((), ())),
                                    preferred_element_type=F32)
                m = jnp.max(s, axis=0, keepdims=True)
                w = jnp.exp2((s - m) * SCALE).astype(BF16)
                r = dot(vt[h], w)
                at = pl.ds(pl.multiple_of(h * HEAD_DIM, HEAD_DIM), HEAD_DIM)
                oref[k, at, :] = r[:HEAD_DIM].astype(BF16)
                sref[k, pl.ds(h, 1), :] = m * SCALE
                sref[k, pl.ds(heads + h, 1), :] = r[HEAD_DIM:HEAD_DIM + 1]
        each(0, heads // 2, pair_step)

    def part_to_x(ap):
        return (send(part.at[ap], xin.at[ap], p_xs.at[ap], p_xr.at[ap], cell=across),
                send(part_s.at[ap], xin_s.at[ap], ps_xs.at[ap], ps_xr.at[ap], cell=across))

    def own_to_z(ap, src):
        to = {"cell": ap * 2 + b}
        return (send(own.at[ap], zin.at[src], p_zs.at[ap], p_zr.at[src], **to),
                send(own_s.at[ap], zin_s.at[src], ps_zs.at[ap], ps_zr.at[src], **to))

    def weights_of(s1, s2):
        m1, l1, m2, l2 = s1[:heads], s1[heads:], s2[:heads], s2[heads:]
        m = jnp.maximum(m1, m2)
        e1, e2 = jnp.exp2(m1 - m), jnp.exp2(m2 - m)
        return e1, e2, jnp.concatenate([m, l1 * e1 + l2 * e2], axis=0)

    def spans():
        return [slice(h * HEAD_DIM, (h + 1) * HEAD_DIM) for h in range(heads)]

    def combine_and_send(d):
        ap = peer(d)
        for c in part_to_x(ap):
            c.wait_recv()
        e1, e2, stat = weights_of(own_s[ap], xin_s[ap])
        own_s[ap] = stat
        for h, at in enumerate(spans()):
            own[ap, at, :] = (own[ap, at, :].astype(F32) * e1[h:h + 1]
                              + xin[ap, at, :].astype(F32) * e2[h:h + 1]).astype(BF16)
        for c in own_to_z(ap, a):
            c.start()

    if na > 1:
        forward(q, q_xs, q_r, 1)
    attend(me, own, own_s, a)

    def step(d):
        ap = peer(d)
        arrived(q, q_xs, q_r, ap * 2 + 1 - b)
        attend(ap * 2 + 1 - b, part, part_s, ap)
        for c in part_to_x(ap):
            c.start()

        @pl.when(d + 1 < na)
        def _():
            forward(q, q_xs, q_r, d + 1)

        attend(ap * 2 + b, own, own_s, ap)

        @pl.when(d > 1)
        def _():
            combine_and_send(d - 1)

    each(1, na, step)
    arrived(q, q_xs, q_r, across)
    if na > 1:
        combine_and_send(na - 1)
    attend(across, part, part_s, a)
    for c in part_to_x(a):
        c.start()

    for at in spans():
        acc[at, :] = own[a, at, :].astype(F32)

    def merge(o_ref, s_ref, k):
        e1, e2, stat = weights_of(own_s[a], s_ref[k])
        own_s[a] = stat
        for h, at in enumerate(spans()):
            acc[at, :] = acc[at, :] * e1[h:h + 1] + o_ref[k, at, :].astype(F32) * e2[h:h + 1]

    def from_z(d):
        ap = peer(na - d)
        for c in own_to_z(ap, ap):
            c.wait_recv()
        merge(zin, zin_s, ap)

    each(1, na, from_z)
    for c in part_to_x(a):
        c.wait_recv()
    merge(xin, xin_s, a)
    totals = own_s[a, heads:, :]
    for h, at in enumerate(spans()):
        acc[at, :] = acc[at, :] / totals[h:h + 1]
    att[...] = acc[...].T.astype(BF16).reshape(2, half, width)

    swap = send(att.at[1 - head], att_in, a_sem.at[0], a_sem.at[1], head=1 - head)
    swap.start()
    own_rows = pl.ds(pl.multiple_of(head * half, half), half)
    first = pl.ds(pl.multiple_of(head * width, width), width)
    second = pl.ds(pl.multiple_of((1 - head) * width, width), width)
    projected = dot(att[head], wo_ref[first, :])
    swap.wait_recv()
    projected = projected + dot(att_in[...], wo_ref[second, :])
    updated = (lat_ref[own_rows, :].astype(F32) + projected).astype(BF16).astype(F32)
    upd[...] = updated
    nrm[me] = (updated * lax.rsqrt(jnp.mean(updated * updated, axis=1, keepdims=True) + 1e-5)
               ).astype(BF16)

    gather_start(nrm, n_zs, n_xs, n_r)
    up_copy.wait_recv()
    down_copy.wait_recv()

    def mlp(slot):
        x = nrm[slot]
        h1 = jax.nn.gelu(dot(x, wu_ref[...]), approximate=True).astype(BF16)
        h2 = jax.nn.gelu(dot(x, wus[...]), approximate=True).astype(BF16)
        return dot(h1, wd_ref[...]) + dot(h2, wds[...])

    def mlp_to_x(ap):
        return send(mpart.at[ap], mxin.at[ap], m_xs.at[ap], m_xr.at[ap], cell=across)

    def mlp_to_z(ap, src):
        return send(mown.at[ap], mzin.at[src], m_zs.at[ap], m_zr.at[src], cell=ap * 2 + b)

    def mlp_combine(d):
        ap = peer(d)
        mlp_to_x(ap).wait_recv()
        mown[ap] = (mown[ap].astype(F32) + mxin[ap].astype(F32)).astype(BF16)
        mlp_to_z(ap, a).start()

    macc[...] = upd[...] + mlp(me)

    def mlp_step(d):
        ap = peer(d)
        forward(nrm, n_xs, n_r, d)
        mown[ap] = mlp(ap * 2 + b).astype(BF16)
        arrived(nrm, n_xs, n_r, ap * 2 + 1 - b)
        mpart[ap] = mlp(ap * 2 + 1 - b).astype(BF16)
        mlp_to_x(ap).start()

        @pl.when(d > 1)
        def _():
            mlp_combine(d - 1)

    each(1, na, mlp_step)
    arrived(nrm, n_xs, n_r, across)
    mpart[a] = mlp(across).astype(BF16)
    mlp_to_x(a).start()
    if na > 1:
        mlp_combine(na - 1)
    mlp_to_x(a).wait_recv()
    macc[...] += mxin[a].astype(F32)

    def mlp_from_z(d):
        ap = peer(na - d)
        mlp_to_z(ap, ap).wait_recv()
        macc[...] += mzin[ap].astype(F32)

    each(1, na, mlp_from_z)
    out_ref[...] = macc[...].astype(BF16)

    gather_finish(q, q_zs, q_xs, q_r)
    gather_finish(nrm, n_zs, n_xs, n_r)
    up_copy.wait_send()
    down_copy.wait_send()
    swap.wait_send()

    def drain_x(ap):
        for c in part_to_x(ap):
            c.wait_send()
        mlp_to_x(ap).wait_send()

    def drain_z(d):
        for c in own_to_z(peer(d), a):
            c.wait_send()
        mlp_to_z(peer(d), a).wait_send()

    each(0, na, drain_x)
    each(1, na, drain_z)


def body(latents, cells, w_query, w_key, w_value, w_out, w_up, w_down):
    n = lax.axis_size("cell")
    na = n // 2
    rows, dim = latents.shape
    half = rows // lax.axis_size("head")
    width = w_query.shape[1]
    heads = width // HEAD_DIM
    count = cells.shape[0]
    vmem = pl.BlockSpec(memory_space=pltpu.VMEM)
    dma = pltpu.SemaphoreType.DMA
    partial = pltpu.VMEM((na, width, rows), BF16)
    stats = pltpu.VMEM((na, 2 * heads, rows), F32)
    mlp_part = pltpu.VMEM((na, half, dim), BF16)
    return pl.pallas_call(
        functools.partial(kernel, n),
        out_shape=jax.ShapeDtypeStruct((half, dim), BF16),
        in_specs=[vmem] * 8,
        out_specs=vmem,
        scratch_shapes=[
            pltpu.VMEM((n, rows, width), BF16),
            pltpu.VMEM((heads, count, PAIR), BF16),
            pltpu.VMEM((heads, HEAD_DIM + EXTRA, count), BF16),
            pltpu.VMEM(w_up.shape, BF16),
            pltpu.VMEM(w_down.shape, BF16),
            partial, partial, partial, partial,
            stats, stats, stats, stats,
            pltpu.VMEM((width, rows), F32),
            pltpu.VMEM((2, half, width), BF16),
            pltpu.VMEM((half, width), BF16),
            pltpu.VMEM((half, dim), F32),
            pltpu.VMEM((n, half, dim), BF16),
            mlp_part, mlp_part, mlp_part, mlp_part,
            pltpu.VMEM((half, dim), F32),
            dma((4,)), dma((na,)), dma((na,)), dma((n,)),
            dma((na,)), dma((na,)), dma((na,)), dma((na,)),
            dma((na,)), dma((na,)), dma((na,)), dma((na,)),
            dma((2,)), dma((na,)), dma((na,)), dma((n,)),
            dma((na,)), dma((na,)), dma((na,)), dma((na,)),
        ],
        compiler_params=pltpu.CompilerParams(
            collective_id=0, has_side_effects=True, vmem_limit_bytes=58 * 1024 * 1024
        ),
        cost_estimate=pl.CostEstimate(
            flops=12_000_000_000, bytes_accessed=9_000_000, transcendentals=17_000_000
        ),
    )(latents, cells, w_query, w_key, w_value, w_out, w_up, w_down)


def solution(mesh):
    return jax.shard_map(
        body,
        mesh=mesh,
        in_specs=(
            P(("group", "cell"), None),
            P(("group", "cell"), None),
            P(None, "head"),
            P(None, "head"),
            P(None, "head"),
            P(),
            P(None, ("cell", "head")),
            P(("cell", "head"), None),
        ),
        out_specs=P(("group", "cell", "head"), None),
        check_vma=False,
    )
```

```python
import functools
import math

import jax
import jax.numpy as jnp
from jax import lax
from jax.experimental import pallas as pl
from jax.experimental.pallas import tpu as pltpu
from jax.sharding import PartitionSpec as P

HEAD_DIM = 64
PAIR = 2 * HEAD_DIM
EXTRA = 16
F32 = jnp.float32
BF16 = jnp.bfloat16
SCALE = HEAD_DIM ** (-0.5) * math.log2(math.e)


def dot(a, b):
    return jnp.dot(a, b, preferred_element_type=F32)


def kernel(
    n,
    lat_ref, cells_ref, wq_ref, wk_ref, wv_ref, wo_ref, wu_ref, wd_ref, out_ref,
    q, cin, kz, vt, wus, wds,
    own, part, zin, own_s, part_s, zin_s,
    acc, att, att_in, nrm, mown, mzin, macc,
    c_sem, w_sem, q_s, q_r, p_s, p_r, ps_s, ps_r, a_sem, n_s, n_r, m_s, m_r,
):
    na = n // 2
    me = lax.axis_index("cell")
    head = lax.axis_index("head")
    a, b = me // 2, me % 2
    across = a * 2 + 1 - b
    heads = wq_ref.shape[1] // HEAD_DIM
    width = wq_ref.shape[1]
    half = out_ref.shape[0]
    count = cells_ref.shape[0]

    def peer(d):
        return (a + d) % na

    def send(src, dst, ss, rs, **where):
        return pltpu.make_async_remote_copy(
            src_ref=src, dst_ref=dst, send_sem=ss, recv_sem=rs,
            device_id=where, device_id_type=pl.DeviceIdType.MESH,
        )

    def each(low, high, f):
        def step(i, carry):
            f(i)
            return carry
        lax.fori_loop(low, high, step, 0)

    barrier = pltpu.get_barrier_semaphore()
    each(1, na, lambda d: pl.semaphore_signal(
        barrier, inc=1, device_id={"cell": peer(d) * 2 + b},
        device_id_type=pl.DeviceIdType.MESH))
    pl.semaphore_signal(barrier, inc=1, device_id={"cell": across},
                        device_id_type=pl.DeviceIdType.MESH)
    pl.semaphore_signal(barrier, inc=1, device_id={"head": 1 - head},
                        device_id_type=pl.DeviceIdType.MESH)
    q[a] = dot(lat_ref[...], wq_ref[...]).astype(BF16)
    pl.semaphore_wait(barrier, na + 1)

    def across_x(src, dst, ss, rs):
        return send(src, dst, ss, rs, cell=across)

    def to_sibling(src, dst, ss, rs):
        return send(src, dst, ss, rs, head=1 - head)

    cell_half = count // 2
    cell_rows = pl.ds(pl.multiple_of(head * cell_half, cell_half), cell_half)
    cells_x = across_x(cells_ref.at[cell_rows], cin.at[head], c_sem.at[0], c_sem.at[1])
    cells_fwd = to_sibling(cin.at[head], cin.at[head], c_sem.at[2], c_sem.at[3])
    cells_from = to_sibling(cin.at[1 - head], cin.at[1 - head], c_sem.at[2], c_sem.at[3])
    up_s = to_sibling(wu_ref, wus.at[0], w_sem.at[0], w_sem.at[1])
    down_s = to_sibling(wd_ref, wds.at[0], w_sem.at[2], w_sem.at[3])
    up_x = across_x(wu_ref, wus.at[1], w_sem.at[4], w_sem.at[5])
    down_x = across_x(wd_ref, wds.at[1], w_sem.at[6], w_sem.at[7])
    up_f = to_sibling(wus.at[1], wus.at[2], w_sem.at[8], w_sem.at[9])
    down_f = to_sibling(wds.at[1], wds.at[2], w_sem.at[10], w_sem.at[11])

    def to_z(buf, ss, r, d):
        return send(buf.at[a], buf.at[a], ss.at[d], r.at[a], cell=peer(d) * 2 + b)

    def arrived(buf, r, ap):
        send(buf.at[ap], buf.at[ap], r.at[ap], r.at[ap], cell=across).wait_recv()

    cells_x.start()
    each(1, na, lambda d: to_z(q, q_s, q_r, d).start())
    up_s.start()
    down_s.start()

    tile = 256

    def project(block, t, side):
        rows = pl.ds(pl.multiple_of(t * tile, tile), tile)
        k = dot(block, wk_ref[...]).astype(BF16)
        v = dot(block, wv_ref[...]).T.astype(BF16)
        lane = lax.broadcasted_iota(jnp.int32, (tile, PAIR), 1)
        for h in range(heads):
            pair = k[:, (h // 2) * PAIR:(h // 2 + 1) * PAIR]
            keep = (lane < HEAD_DIM) if h % 2 == 0 else (lane >= HEAD_DIM)
            kz[side * heads + h, rows, :] = jnp.where(keep, pair, jnp.zeros_like(pair))
            vt[side * heads + h, :HEAD_DIM, rows] = v[h * HEAD_DIM:(h + 1) * HEAD_DIM, :]
            vt[side * heads + h, HEAD_DIM:, rows] = jnp.ones((EXTRA, tile), BF16)

    def rows_at(t):
        return pl.ds(pl.multiple_of(t * tile, tile), tile)

    each(0, count // tile, lambda t: project(cells_ref[rows_at(t), :], t, 0))

    def attend(side, oref, sref, k):
        def pair_step(p):
            q2 = q[k, :, pl.ds(pl.multiple_of(p * PAIR, PAIR), PAIR)]
            for e in range(2):
                h = 2 * p + e
                s = lax.dot_general(kz[side * heads + h], q2, (((1,), (1,)), ((), ())),
                                    preferred_element_type=F32)
                m = jnp.max(s, axis=0, keepdims=True)
                w = jnp.exp2((s - m) * SCALE).astype(BF16)
                r = dot(vt[side * heads + h], w)
                at = pl.ds(pl.multiple_of(h * HEAD_DIM, HEAD_DIM), HEAD_DIM)
                oref[k, at, :] = r[:HEAD_DIM].astype(BF16)
                sref[k, pl.ds(h, 1), :] = m * SCALE
                sref[k, pl.ds(heads + h, 1), :] = r[HEAD_DIM:HEAD_DIM + 1]
        each(0, heads // 2, pair_step)

    def own_to_z(ap, src):
        to = {"cell": ap * 2 + b}
        return (send(own.at[ap], zin.at[src], p_s.at[ap], p_r.at[src], **to),
                send(own_s.at[ap], zin_s.at[src], ps_s.at[ap], ps_r.at[src], **to))

    def weights_of(s1, s2):
        m1, l1, m2, l2 = s1[:heads], s1[heads:], s2[:heads], s2[heads:]
        m = jnp.maximum(m1, m2)
        e1, e2 = jnp.exp2(m1 - m), jnp.exp2(m2 - m)
        return e1, e2, jnp.concatenate([m, l1 * e1 + l2 * e2], axis=0)

    def spans():
        return [slice(h * HEAD_DIM, (h + 1) * HEAD_DIM) for h in range(heads)]

    attend(0, own, own_s, a)

    def first_side(d):
        ap = peer(d)
        arrived(q, q_r, ap)
        attend(0, own, own_s, ap)

        @pl.when(d == 1)
        def _():
            cells_x.wait_recv()
            cells_fwd.start()
            up_x.start()
            down_x.start()

    each(1, na, first_side)

    def project_in(i):
        side = i // (cell_half // tile)
        at = i % (cell_half // tile)
        project(cin[side, rows_at(at), :], i, 1)

    cells_from.wait_recv()
    each(0, count // tile, project_in)

    def second_side(d):
        ap = peer(d)
        attend(1, part, part_s, ap)
        e1, e2, stat = weights_of(own_s[ap], part_s[ap])
        own_s[ap] = stat
        for h, at in enumerate(spans()):
            own[ap, at, :] = (own[ap, at, :].astype(F32) * e1[h:h + 1]
                              + part[ap, at, :].astype(F32) * e2[h:h + 1]).astype(BF16)
        for c in own_to_z(ap, a):
            c.start()

    each(1, na, second_side)
    up_x.wait_recv()
    down_x.wait_recv()
    up_f.start()
    down_f.start()
    attend(1, part, part_s, a)

    for at in spans():
        acc[at, :] = own[a, at, :].astype(F32)

    def merge(o_ref, s_ref, k):
        e1, e2, stat = weights_of(own_s[a], s_ref[k])
        own_s[a] = stat
        for h, at in enumerate(spans()):
            acc[at, :] = acc[at, :] * e1[h:h + 1] + o_ref[k, at, :].astype(F32) * e2[h:h + 1]

    merge(part, part_s, a)

    def from_z(d):
        ap = peer(na - d)
        for c in own_to_z(ap, ap):
            c.wait_recv()
        merge(zin, zin_s, ap)

    each(1, na, from_z)
    totals = own_s[a, heads:, :]
    for h, at in enumerate(spans()):
        acc[at, :] = acc[at, :] / totals[h:h + 1]
    att[...] = acc[...].T.astype(BF16).reshape(2, half, width)

    swap = to_sibling(att.at[1 - head], att_in, a_sem.at[0], a_sem.at[1])
    swap.start()
    own_rows = pl.ds(pl.multiple_of(head * half, half), half)
    first = pl.ds(pl.multiple_of(head * width, width), width)
    second = pl.ds(pl.multiple_of((1 - head) * width, width), width)
    projected = dot(att[head], wo_ref[first, :])
    swap.wait_recv()
    projected = projected + dot(att_in[...], wo_ref[second, :])
    updated = (lat_ref[own_rows, :].astype(F32) + projected).astype(BF16).astype(F32)
    macc[...] = updated
    nrm[a] = (updated * lax.rsqrt(jnp.mean(updated * updated, axis=1, keepdims=True) + 1e-5)
              ).astype(BF16)
    each(1, na, lambda d: to_z(nrm, n_s, n_r, d).start())
    for c in (up_s, down_s, up_f, down_f):
        c.wait_recv()

    def mlp(slot):
        x = nrm[slot]
        hid = jax.nn.gelu(dot(x, wu_ref[...]), approximate=True).astype(BF16)
        total = dot(hid, wd_ref[...])
        for i in range(3):
            hid = jax.nn.gelu(dot(x, wus[i]), approximate=True).astype(BF16)
            total = total + dot(hid, wds[i])
        return total

    def mlp_to_z(ap, src):
        return send(mown.at[ap], mzin.at[src], m_s.at[ap], m_r.at[src], cell=ap * 2 + b)

    def mlp_step(d):
        ap = peer(d)
        arrived(nrm, n_r, ap)
        mown[ap] = mlp(ap).astype(BF16)
        mlp_to_z(ap, a).start()

    macc[...] += mlp(a)
    each(1, na, mlp_step)

    def mlp_from_z(d):
        ap = peer(na - d)
        mlp_to_z(ap, ap).wait_recv()
        macc[...] += mzin[ap].astype(F32)

    each(1, na, mlp_from_z)
    out_ref[...] = macc[...].astype(BF16)

    for c in (cells_x, cells_fwd, up_s, down_s, up_x, down_x, up_f, down_f, swap):
        c.wait_send()

    def drain(d):
        to_z(q, q_s, q_r, d).wait_send()
        to_z(nrm, n_s, n_r, d).wait_send()
        for c in own_to_z(peer(d), a):
            c.wait_send()
        mlp_to_z(peer(d), a).wait_send()

    each(1, na, drain)


def body(latents, cells, w_query, w_key, w_value, w_out, w_up, w_down):
    n = lax.axis_size("cell")
    na = n // 2
    rows, dim = latents.shape
    half = rows // lax.axis_size("head")
    width = w_query.shape[1]
    heads = width // HEAD_DIM
    count = cells.shape[0]
    vmem = pl.BlockSpec(memory_space=pltpu.VMEM)
    dma = pltpu.SemaphoreType.DMA
    partial = pltpu.VMEM((na, width, rows), BF16)
    stats = pltpu.VMEM((na, 2 * heads, rows), F32)
    mlp_part = pltpu.VMEM((na, half, dim), BF16)
    return pl.pallas_call(
        functools.partial(kernel, n),
        out_shape=jax.ShapeDtypeStruct((half, dim), BF16),
        in_specs=[vmem] * 8,
        out_specs=vmem,
        scratch_shapes=[
            pltpu.VMEM((na, rows, width), BF16),
            pltpu.VMEM((2, count // 2, dim), BF16),
            pltpu.VMEM((2 * heads, count, PAIR), BF16),
            pltpu.VMEM((2 * heads, HEAD_DIM + EXTRA, count), BF16),
            pltpu.VMEM((3,) + w_up.shape, BF16),
            pltpu.VMEM((3,) + w_down.shape, BF16),
            partial, partial, partial,
            stats, stats, stats,
            pltpu.VMEM((width, rows), F32),
            pltpu.VMEM((2, half, width), BF16),
            pltpu.VMEM((half, width), BF16),
            pltpu.VMEM((na, half, dim), BF16),
            mlp_part, mlp_part,
            pltpu.VMEM((half, dim), F32),
            dma((4,)), dma((12,)), dma((na,)), dma((na,)),
            dma((na,)), dma((na,)), dma((na,)), dma((na,)), dma((2,)),
            dma((na,)), dma((na,)), dma((na,)), dma((na,)),
        ],
        compiler_params=pltpu.CompilerParams(
            collective_id=0, has_side_effects=True, vmem_limit_bytes=58 * 1024 * 1024
        ),
        cost_estimate=pl.CostEstimate(
            flops=12_000_000_000, bytes_accessed=9_000_000, transcendentals=17_000_000
        ),
    )(latents, cells, w_query, w_key, w_value, w_out, w_up, w_down)


def solution(mesh):
    return jax.shard_map(
        body,
        mesh=mesh,
        in_specs=(
            P(("group", "cell"), None),
            P(("group", "cell"), None),
            P(None, "head"),
            P(None, "head"),
            P(None, "head"),
            P(),
            P(None, ("cell", "head")),
            P(("cell", "head"), None),
        ),
        out_specs=P(("group", "cell", "head"), None),
        check_vma=False,
    )
```

```python
import functools
import math

import jax
import jax.numpy as jnp
from jax import lax
from jax.experimental import pallas as pl
from jax.experimental.pallas import tpu as pltpu
from jax.sharding import PartitionSpec as P

HEAD_DIM = 64
PAIR = 2 * HEAD_DIM
EXTRA = 16
F32 = jnp.float32
BF16 = jnp.bfloat16
SCALE = HEAD_DIM ** (-0.5) * math.log2(math.e)


def dot(a, b):
    return jnp.dot(a, b, preferred_element_type=F32)


def kernel(
    n,
    lat_ref, cells_ref, wq_ref, wk_ref, wv_ref, wo_ref, wu_ref, wd_ref, out_ref,
    q, cin, kz, vt, wus, wds,
    own, part, zin, own_s, part_s, zin_s,
    acc, att, att_in, nrm, mown, mzin, macc,
    c_sem, w_sem, q_s, q_r, p_s, p_r, ps_s, ps_r, a_sem, n_s, n_r, m_s, m_r,
):
    na = n // 2
    me = lax.axis_index("cell")
    head = lax.axis_index("head")
    a, b = me // 2, me % 2
    across = a * 2 + 1 - b
    heads = wq_ref.shape[1] // HEAD_DIM
    width = wq_ref.shape[1]
    half = out_ref.shape[0]
    count = cells_ref.shape[0]

    def peer(d):
        return (a + d) % na

    def send(src, dst, ss, rs, **where):
        return pltpu.make_async_remote_copy(
            src_ref=src, dst_ref=dst, send_sem=ss, recv_sem=rs,
            device_id=where, device_id_type=pl.DeviceIdType.MESH,
        )

    def each(low, high, f):
        def step(i, carry):
            f(i)
            return carry
        lax.fori_loop(low, high, step, 0)

    barrier = pltpu.get_barrier_semaphore()
    each(1, na, lambda d: pl.semaphore_signal(
        barrier, inc=1, device_id={"cell": peer(d) * 2 + b},
        device_id_type=pl.DeviceIdType.MESH))
    pl.semaphore_signal(barrier, inc=1, device_id={"cell": across},
                        device_id_type=pl.DeviceIdType.MESH)
    pl.semaphore_signal(barrier, inc=1, device_id={"head": 1 - head},
                        device_id_type=pl.DeviceIdType.MESH)
    q[a] = dot(lat_ref[...], wq_ref[...]).astype(BF16)
    pl.semaphore_wait(barrier, na + 1)

    def across_x(src, dst, ss, rs):
        return send(src, dst, ss, rs, cell=across)

    def to_sibling(src, dst, ss, rs):
        return send(src, dst, ss, rs, head=1 - head)

    cell_half = count // 2
    cell_rows = pl.ds(pl.multiple_of(head * cell_half, cell_half), cell_half)
    cells_x = across_x(cells_ref.at[cell_rows], cin.at[head], c_sem.at[0], c_sem.at[1])
    cells_fwd = to_sibling(cin.at[head], cin.at[head], c_sem.at[2], c_sem.at[3])
    cells_from = to_sibling(cin.at[1 - head], cin.at[1 - head], c_sem.at[2], c_sem.at[3])
    up_s = to_sibling(wu_ref, wus.at[0], w_sem.at[0], w_sem.at[1])
    down_s = to_sibling(wd_ref, wds.at[0], w_sem.at[2], w_sem.at[3])
    up_x = across_x(wu_ref, wus.at[1], w_sem.at[4], w_sem.at[5])
    down_x = across_x(wd_ref, wds.at[1], w_sem.at[6], w_sem.at[7])
    up_f = to_sibling(wus.at[1], wus.at[2], w_sem.at[8], w_sem.at[9])
    down_f = to_sibling(wds.at[1], wds.at[2], w_sem.at[10], w_sem.at[11])

    def up_z(buf, ss, r, j):
        return send(buf.at[j], buf.at[j], ss.at[j], r.at[j], cell=me + 2)

    def down_z(buf, ss, r, j):
        return send(buf.at[j], buf.at[j], ss.at[na + j], r.at[j], cell=me - 2)

    def pass_on(buf, ss, r, j, rising, falling):
        if rising:
            @pl.when(a + 1 < na)
            def _():
                up_z(buf, ss, r, j).start()
        if falling:
            @pl.when(a > 0)
            def _():
                down_z(buf, ss, r, j).start()

    def line_step(buf, ss, r, k, work):
        @pl.when(a >= k)
        def _():
            arrived(buf, r, a - k)
            pass_on(buf, ss, r, a - k, True, False)

        @pl.when(a + k < na)
        def _():
            arrived(buf, r, a + k)
            pass_on(buf, ss, r, a + k, False, True)

        pl.when(a >= k)(lambda: work(a - k))
        pl.when(a + k < na)(lambda: work(a + k))

    def line_finish(buf, ss, r):
        @pl.when(a + 1 < na)
        def _():
            each(0, a + 1, lambda j: up_z(buf, ss, r, j).wait_send())

        @pl.when(a > 0)
        def _():
            each(a, na, lambda j: down_z(buf, ss, r, j).wait_send())

    def arrived(buf, r, ap):
        send(buf.at[ap], buf.at[ap], r.at[ap], r.at[ap], cell=across).wait_recv()

    cells_x.start()
    pass_on(q, q_s, q_r, a, True, True)
    up_s.start()
    down_s.start()

    tile = 256

    def project(block, t, side):
        rows = pl.ds(pl.multiple_of(t * tile, tile), tile)
        k = dot(block, wk_ref[...]).astype(BF16)
        v = dot(block, wv_ref[...]).T.astype(BF16)
        lane = lax.broadcasted_iota(jnp.int32, (tile, PAIR), 1)
        for h in range(heads):
            pair = k[:, (h // 2) * PAIR:(h // 2 + 1) * PAIR]
            keep = (lane < HEAD_DIM) if h % 2 == 0 else (lane >= HEAD_DIM)
            kz[side * heads + h, rows, :] = jnp.where(keep, pair, jnp.zeros_like(pair))
            vt[side * heads + h, :HEAD_DIM, rows] = v[h * HEAD_DIM:(h + 1) * HEAD_DIM, :]
            vt[side * heads + h, HEAD_DIM:, rows] = jnp.ones((EXTRA, tile), BF16)

    def rows_at(t):
        return pl.ds(pl.multiple_of(t * tile, tile), tile)

    each(0, count // tile, lambda t: project(cells_ref[rows_at(t), :], t, 0))

    def attend(side, oref, sref, k):
        def pair_step(p):
            q2 = q[k, :, pl.ds(pl.multiple_of(p * PAIR, PAIR), PAIR)]
            for e in range(2):
                h = 2 * p + e
                s = lax.dot_general(kz[side * heads + h], q2, (((1,), (1,)), ((), ())),
                                    preferred_element_type=F32)
                m = jnp.max(s, axis=0, keepdims=True)
                w = jnp.exp2((s - m) * SCALE).astype(BF16)
                r = dot(vt[side * heads + h], w)
                at = pl.ds(pl.multiple_of(h * HEAD_DIM, HEAD_DIM), HEAD_DIM)
                oref[k, at, :] = r[:HEAD_DIM].astype(BF16)
                sref[k, pl.ds(h, 1), :] = m * SCALE
                sref[k, pl.ds(heads + h, 1), :] = r[HEAD_DIM:HEAD_DIM + 1]
        each(0, heads // 2, pair_step)

    def own_to_z(ap, src):
        to = {"cell": ap * 2 + b}
        return (send(own.at[ap], zin.at[src], p_s.at[ap], p_r.at[src], **to),
                send(own_s.at[ap], zin_s.at[src], ps_s.at[ap], ps_r.at[src], **to))

    def weights_of(s1, s2):
        m1, l1, m2, l2 = s1[:heads], s1[heads:], s2[:heads], s2[heads:]
        m = jnp.maximum(m1, m2)
        e1, e2 = jnp.exp2(m1 - m), jnp.exp2(m2 - m)
        return e1, e2, jnp.concatenate([m, l1 * e1 + l2 * e2], axis=0)

    def spans():
        return [slice(h * HEAD_DIM, (h + 1) * HEAD_DIM) for h in range(heads)]

    attend(0, own, own_s, a)

    each(1, na, lambda k: line_step(q, q_s, q_r, k, lambda j: attend(0, own, own_s, j)))
    cells_x.wait_recv()
    cells_fwd.start()
    up_x.start()
    down_x.start()

    def project_in(i):
        side = i // (cell_half // tile)
        at = i % (cell_half // tile)
        project(cin[side, rows_at(at), :], i, 1)

    cells_from.wait_recv()
    each(0, count // tile, project_in)

    def second_side(d):
        ap = peer(d)
        attend(1, part, part_s, ap)
        e1, e2, stat = weights_of(own_s[ap], part_s[ap])
        own_s[ap] = stat
        for h, at in enumerate(spans()):
            own[ap, at, :] = (own[ap, at, :].astype(F32) * e1[h:h + 1]
                              + part[ap, at, :].astype(F32) * e2[h:h + 1]).astype(BF16)
        for c in own_to_z(ap, a):
            c.start()

    each(1, na, second_side)
    up_x.wait_recv()
    down_x.wait_recv()
    up_f.start()
    down_f.start()
    attend(1, part, part_s, a)

    for at in spans():
        acc[at, :] = own[a, at, :].astype(F32)

    def merge(o_ref, s_ref, k):
        e1, e2, stat = weights_of(own_s[a], s_ref[k])
        own_s[a] = stat
        for h, at in enumerate(spans()):
            acc[at, :] = acc[at, :] * e1[h:h + 1] + o_ref[k, at, :].astype(F32) * e2[h:h + 1]

    merge(part, part_s, a)

    def from_z(d):
        ap = peer(na - d)
        for c in own_to_z(ap, ap):
            c.wait_recv()
        merge(zin, zin_s, ap)

    each(1, na, from_z)
    totals = own_s[a, heads:, :]
    for h, at in enumerate(spans()):
        acc[at, :] = acc[at, :] / totals[h:h + 1]
    att[...] = acc[...].T.astype(BF16).reshape(2, half, width)

    swap = to_sibling(att.at[1 - head], att_in, a_sem.at[0], a_sem.at[1])
    swap.start()
    own_rows = pl.ds(pl.multiple_of(head * half, half), half)
    first = pl.ds(pl.multiple_of(head * width, width), width)
    second = pl.ds(pl.multiple_of((1 - head) * width, width), width)
    projected = dot(att[head], wo_ref[first, :])
    swap.wait_recv()
    projected = projected + dot(att_in[...], wo_ref[second, :])
    updated = (lat_ref[own_rows, :].astype(F32) + projected).astype(BF16).astype(F32)
    macc[...] = updated
    nrm[a] = (updated * lax.rsqrt(jnp.mean(updated * updated, axis=1, keepdims=True) + 1e-5)
              ).astype(BF16)
    pass_on(nrm, n_s, n_r, a, True, True)
    for c in (up_s, down_s, up_f, down_f):
        c.wait_recv()

    def mlp(slot):
        x = nrm[slot]
        hid = jax.nn.gelu(dot(x, wu_ref[...]), approximate=True).astype(BF16)
        total = dot(hid, wd_ref[...])
        for i in range(3):
            hid = jax.nn.gelu(dot(x, wus[i]), approximate=True).astype(BF16)
            total = total + dot(hid, wds[i])
        return total

    def mlp_to_z(ap, src):
        return send(mown.at[ap], mzin.at[src], m_s.at[ap], m_r.at[src], cell=ap * 2 + b)

    def mlp_step(ap):
        mown[ap] = mlp(ap).astype(BF16)
        mlp_to_z(ap, a).start()

    macc[...] += mlp(a)
    each(1, na, lambda k: line_step(nrm, n_s, n_r, k, mlp_step))

    def mlp_from_z(d):
        ap = peer(na - d)
        mlp_to_z(ap, ap).wait_recv()
        macc[...] += mzin[ap].astype(F32)

    each(1, na, mlp_from_z)
    out_ref[...] = macc[...].astype(BF16)

    for c in (cells_x, cells_fwd, up_s, down_s, up_x, down_x, up_f, down_f, swap):
        c.wait_send()

    def drain(d):
        for c in own_to_z(peer(d), a):
            c.wait_send()
        mlp_to_z(peer(d), a).wait_send()

    each(1, na, drain)
    line_finish(q, q_s, q_r)
    line_finish(nrm, n_s, n_r)


def body(latents, cells, w_query, w_key, w_value, w_out, w_up, w_down):
    n = lax.axis_size("cell")
    na = n // 2
    rows, dim = latents.shape
    half = rows // lax.axis_size("head")
    width = w_query.shape[1]
    heads = width // HEAD_DIM
    count = cells.shape[0]
    vmem = pl.BlockSpec(memory_space=pltpu.VMEM)
    dma = pltpu.SemaphoreType.DMA
    partial = pltpu.VMEM((na, width, rows), BF16)
    stats = pltpu.VMEM((na, 2 * heads, rows), F32)
    mlp_part = pltpu.VMEM((na, half, dim), BF16)
    return pl.pallas_call(
        functools.partial(kernel, n),
        out_shape=jax.ShapeDtypeStruct((half, dim), BF16),
        in_specs=[vmem] * 8,
        out_specs=vmem,
        scratch_shapes=[
            pltpu.VMEM((na, rows, width), BF16),
            pltpu.VMEM((2, count // 2, dim), BF16),
            pltpu.VMEM((2 * heads, count, PAIR), BF16),
            pltpu.VMEM((2 * heads, HEAD_DIM + EXTRA, count), BF16),
            pltpu.VMEM((3,) + w_up.shape, BF16),
            pltpu.VMEM((3,) + w_down.shape, BF16),
            partial, partial, partial,
            stats, stats, stats,
            pltpu.VMEM((width, rows), F32),
            pltpu.VMEM((2, half, width), BF16),
            pltpu.VMEM((half, width), BF16),
            pltpu.VMEM((na, half, dim), BF16),
            mlp_part, mlp_part,
            pltpu.VMEM((half, dim), F32),
            dma((4,)), dma((12,)), dma((2 * na,)), dma((na,)),
            dma((na,)), dma((na,)), dma((na,)), dma((na,)), dma((2,)),
            dma((2 * na,)), dma((na,)), dma((na,)), dma((na,)),
        ],
        compiler_params=pltpu.CompilerParams(
            collective_id=0, has_side_effects=True, vmem_limit_bytes=58 * 1024 * 1024
        ),
        cost_estimate=pl.CostEstimate(
            flops=12_000_000_000, bytes_accessed=9_000_000, transcendentals=17_000_000
        ),
    )(latents, cells, w_query, w_key, w_value, w_out, w_up, w_down)


def solution(mesh):
    return jax.shard_map(
        body,
        mesh=mesh,
        in_specs=(
            P(("group", "cell"), None),
            P(("group", "cell"), None),
            P(None, "head"),
            P(None, "head"),
            P(None, "head"),
            P(),
            P(None, ("cell", "head")),
            P(("cell", "head"), None),
        ),
        out_specs=P(("group", "cell", "head"), None),
        check_vma=False,
    )
```

```python
import functools
import math

import jax
import jax.numpy as jnp
from jax import lax
from jax.experimental import pallas as pl
from jax.experimental.pallas import tpu as pltpu
from jax.sharding import PartitionSpec as P

HEAD_DIM = 64
PAIR = 2 * HEAD_DIM
EXTRA = 16
F32 = jnp.float32
BF16 = jnp.bfloat16
SCALE = HEAD_DIM ** (-0.5) * math.log2(math.e)


def dot(a, b):
    return jnp.dot(a, b, preferred_element_type=F32)


def kernel(
    n,
    lat_ref, cells_ref, wq_ref, wk_ref, wv_ref, wo_ref, wu_ref, wd_ref, out_ref,
    q, cin, kz, vt, wus, wds,
    own, part, zin, own_s, part_s, zin_s,
    acc, att, att_in, nrm, mown, mzin, macc,
    c_sem, w_sem, q_s, q_r, p_s, p_r, ps_s, ps_r, a_sem, n_s, n_r, m_s, m_r,
):
    na = n // 2
    me = lax.axis_index("cell")
    head = lax.axis_index("head")
    a, b = me // 2, me % 2
    across = a * 2 + 1 - b
    heads = wq_ref.shape[1] // HEAD_DIM
    width = wq_ref.shape[1]
    half = out_ref.shape[0]
    count = cells_ref.shape[0]

    def peer(d):
        return (a + d) % na

    def send(src, dst, ss, rs, **where):
        return pltpu.make_async_remote_copy(
            src_ref=src, dst_ref=dst, send_sem=ss, recv_sem=rs,
            device_id=where, device_id_type=pl.DeviceIdType.MESH,
        )

    def each(low, high, f):
        def step(i, carry):
            f(i)
            return carry
        lax.fori_loop(low, high, step, 0)

    barrier = pltpu.get_barrier_semaphore()
    each(1, na, lambda d: pl.semaphore_signal(
        barrier, inc=1, device_id={"cell": peer(d) * 2 + b},
        device_id_type=pl.DeviceIdType.MESH))
    pl.semaphore_signal(barrier, inc=1, device_id={"cell": across},
                        device_id_type=pl.DeviceIdType.MESH)
    pl.semaphore_signal(barrier, inc=1, device_id={"head": 1 - head},
                        device_id_type=pl.DeviceIdType.MESH)
    q[a] = dot(lat_ref[...], wq_ref[...]).astype(BF16)
    pl.semaphore_wait(barrier, na + 1)

    def across_x(src, dst, ss, rs):
        return send(src, dst, ss, rs, cell=across)

    def to_sibling(src, dst, ss, rs):
        return send(src, dst, ss, rs, head=1 - head)

    cell_half = count // 2
    cell_rows = pl.ds(pl.multiple_of(head * cell_half, cell_half), cell_half)
    cells_x = across_x(cells_ref.at[cell_rows], cin.at[head], c_sem.at[0], c_sem.at[1])
    cells_fwd = to_sibling(cin.at[head], cin.at[head], c_sem.at[2], c_sem.at[3])
    cells_from = to_sibling(cin.at[1 - head], cin.at[1 - head], c_sem.at[2], c_sem.at[3])
    up_s = to_sibling(wu_ref, wus.at[0], w_sem.at[0], w_sem.at[1])
    down_s = to_sibling(wd_ref, wds.at[0], w_sem.at[2], w_sem.at[3])
    up_x = across_x(wu_ref, wus.at[1], w_sem.at[4], w_sem.at[5])
    down_x = across_x(wd_ref, wds.at[1], w_sem.at[6], w_sem.at[7])
    up_f = to_sibling(wus.at[1], wus.at[2], w_sem.at[8], w_sem.at[9])
    down_f = to_sibling(wds.at[1], wds.at[2], w_sem.at[10], w_sem.at[11])

    def up_z(buf, ss, r, j):
        return send(buf.at[j], buf.at[j], ss.at[j], r.at[j], cell=me + 2)

    def down_z(buf, ss, r, j):
        return send(buf.at[j], buf.at[j], ss.at[na + j], r.at[j], cell=me - 2)

    def pass_on(buf, ss, r, j, rising, falling):
        if rising:
            @pl.when(a + 1 < na)
            def _():
                up_z(buf, ss, r, j).start()
        if falling:
            @pl.when(a > 0)
            def _():
                down_z(buf, ss, r, j).start()

    def line_step(buf, ss, r, k, work):
        @pl.when(a >= k)
        def _():
            arrived(buf, r, a - k)
            pass_on(buf, ss, r, a - k, True, False)

        @pl.when(a + k < na)
        def _():
            arrived(buf, r, a + k)
            pass_on(buf, ss, r, a + k, False, True)

        pl.when(a >= k)(lambda: work(a - k))
        pl.when(a + k < na)(lambda: work(a + k))

    def line_finish(buf, ss, r):
        @pl.when(a + 1 < na)
        def _():
            each(0, a + 1, lambda j: up_z(buf, ss, r, j).wait_send())

        @pl.when(a > 0)
        def _():
            each(a, na, lambda j: down_z(buf, ss, r, j).wait_send())

    def arrived(buf, r, ap):
        send(buf.at[ap], buf.at[ap], r.at[ap], r.at[ap], cell=across).wait_recv()

    cells_x.start()
    pass_on(q, q_s, q_r, a, True, True)
    up_s.start()
    down_s.start()

    tile = 256

    def project(block, t, side):
        rows = pl.ds(pl.multiple_of(t * tile, tile), tile)
        k = dot(block, wk_ref[...]).astype(BF16)
        v = dot(block, wv_ref[...]).T.astype(BF16)
        lane = lax.broadcasted_iota(jnp.int32, (tile, PAIR), 1)
        for h in range(heads):
            pair = k[:, (h // 2) * PAIR:(h // 2 + 1) * PAIR]
            keep = (lane < HEAD_DIM) if h % 2 == 0 else (lane >= HEAD_DIM)
            kz[side * heads + h, rows, :] = jnp.where(keep, pair, jnp.zeros_like(pair))
            vt[side * heads + h, :HEAD_DIM, rows] = v[h * HEAD_DIM:(h + 1) * HEAD_DIM, :]
            vt[side * heads + h, HEAD_DIM:, rows] = jnp.ones((EXTRA, tile), BF16)

    def rows_at(t):
        return pl.ds(pl.multiple_of(t * tile, tile), tile)

    each(0, count // tile, lambda t: project(cells_ref[rows_at(t), :], t, 0))

    def attend(side, oref, sref, k):
        def pair_step(p):
            q2 = q[k, :, pl.ds(pl.multiple_of(p * PAIR, PAIR), PAIR)]
            for e in range(2):
                h = 2 * p + e
                s = lax.dot_general(kz[side * heads + h], q2, (((1,), (1,)), ((), ())),
                                    preferred_element_type=F32)
                m = jnp.max(s, axis=0, keepdims=True)
                w = jnp.exp2((s - m) * SCALE).astype(BF16)
                r = dot(vt[side * heads + h], w)
                at = pl.ds(pl.multiple_of(h * HEAD_DIM, HEAD_DIM), HEAD_DIM)
                oref[k, at, :] = r[:HEAD_DIM].astype(BF16)
                sref[k, pl.ds(h, 1), :] = m * SCALE
                sref[k, pl.ds(heads + h, 1), :] = r[HEAD_DIM:HEAD_DIM + 1]
        each(0, heads // 2, pair_step)

    def own_to_z(ap, src):
        to = {"cell": ap * 2 + b}
        return (send(own.at[ap], zin.at[src], p_s.at[ap], p_r.at[src], **to),
                send(own_s.at[ap], zin_s.at[src], ps_s.at[ap], ps_r.at[src], **to))

    def weights_of(s1, s2):
        m1, l1, m2, l2 = s1[:heads], s1[heads:], s2[:heads], s2[heads:]
        m = jnp.maximum(m1, m2)
        e1, e2 = jnp.exp2(m1 - m), jnp.exp2(m2 - m)
        return e1, e2, jnp.concatenate([m, l1 * e1 + l2 * e2], axis=0)

    def spans():
        return [slice(h * HEAD_DIM, (h + 1) * HEAD_DIM) for h in range(heads)]

    attend(0, own, own_s, a)

    each(1, na, lambda k: line_step(q, q_s, q_r, k, lambda j: attend(0, own, own_s, j)))
    cells_x.wait_recv()
    cells_fwd.start()
    up_x.start()
    down_x.start()

    def project_in(i):
        side = i // (cell_half // tile)
        at = i % (cell_half // tile)
        project(cin[side, rows_at(at), :], i, 1)

    cells_from.wait_recv()
    each(0, count // tile, project_in)

    def second_side(d):
        ap = (a + jnp.where(a < na // 2, na - d, d)) % na
        attend(1, part, part_s, ap)
        e1, e2, stat = weights_of(own_s[ap], part_s[ap])
        own_s[ap] = stat
        for h, at in enumerate(spans()):
            own[ap, at, :] = (own[ap, at, :].astype(F32) * e1[h:h + 1]
                              + part[ap, at, :].astype(F32) * e2[h:h + 1]).astype(BF16)
        for c in own_to_z(ap, a):
            c.start()

    each(1, na, second_side)
    up_x.wait_recv()
    down_x.wait_recv()
    up_f.start()
    down_f.start()
    attend(1, part, part_s, a)

    for at in spans():
        acc[at, :] = own[a, at, :].astype(F32)

    def merge(o_ref, s_ref, k):
        e1, e2, stat = weights_of(own_s[a], s_ref[k])
        own_s[a] = stat
        for h, at in enumerate(spans()):
            acc[at, :] = acc[at, :] * e1[h:h + 1] + o_ref[k, at, :].astype(F32) * e2[h:h + 1]

    merge(part, part_s, a)

    def from_z(d):
        ap = peer(na - d)
        for c in own_to_z(ap, ap):
            c.wait_recv()
        merge(zin, zin_s, ap)

    each(1, na, from_z)
    totals = own_s[a, heads:, :]
    for h, at in enumerate(spans()):
        acc[at, :] = acc[at, :] / totals[h:h + 1]
    att[...] = acc[...].T.astype(BF16).reshape(2, half, width)

    swap = to_sibling(att.at[1 - head], att_in, a_sem.at[0], a_sem.at[1])
    swap.start()
    own_rows = pl.ds(pl.multiple_of(head * half, half), half)
    first = pl.ds(pl.multiple_of(head * width, width), width)
    second = pl.ds(pl.multiple_of((1 - head) * width, width), width)
    projected = dot(att[head], wo_ref[first, :])
    swap.wait_recv()
    projected = projected + dot(att_in[...], wo_ref[second, :])
    updated = (lat_ref[own_rows, :].astype(F32) + projected).astype(BF16).astype(F32)
    macc[...] = updated
    nrm[a] = (updated * lax.rsqrt(jnp.mean(updated * updated, axis=1, keepdims=True) + 1e-5)
              ).astype(BF16)
    pass_on(nrm, n_s, n_r, a, True, True)
    for c in (up_s, down_s, up_f, down_f):
        c.wait_recv()

    def mlp(slot):
        x = nrm[slot]
        hid = jax.nn.gelu(dot(x, wu_ref[...]), approximate=True).astype(BF16)
        total = dot(hid, wd_ref[...])
        for i in range(3):
            hid = jax.nn.gelu(dot(x, wus[i]), approximate=True).astype(BF16)
            total = total + dot(hid, wds[i])
        return total

    def mlp_to_z(ap, src):
        return send(mown.at[ap], mzin.at[src], m_s.at[ap], m_r.at[src], cell=ap * 2 + b)

    def mlp_step(ap):
        mown[ap] = mlp(ap).astype(BF16)
        mlp_to_z(ap, a).start()

    macc[...] += mlp(a)
    each(1, na, lambda k: line_step(nrm, n_s, n_r, k, mlp_step))

    def mlp_from_z(d):
        ap = peer(na - d)
        mlp_to_z(ap, ap).wait_recv()
        macc[...] += mzin[ap].astype(F32)

    each(1, na, mlp_from_z)
    out_ref[...] = macc[...].astype(BF16)

    for c in (cells_x, cells_fwd, up_s, down_s, up_x, down_x, up_f, down_f, swap):
        c.wait_send()

    def drain(d):
        for c in own_to_z(peer(d), a):
            c.wait_send()
        mlp_to_z(peer(d), a).wait_send()

    each(1, na, drain)
    line_finish(q, q_s, q_r)
    line_finish(nrm, n_s, n_r)


def body(latents, cells, w_query, w_key, w_value, w_out, w_up, w_down):
    n = lax.axis_size("cell")
    na = n // 2
    rows, dim = latents.shape
    half = rows // lax.axis_size("head")
    width = w_query.shape[1]
    heads = width // HEAD_DIM
    count = cells.shape[0]
    vmem = pl.BlockSpec(memory_space=pltpu.VMEM)
    dma = pltpu.SemaphoreType.DMA
    partial = pltpu.VMEM((na, width, rows), BF16)
    stats = pltpu.VMEM((na, 2 * heads, rows), F32)
    mlp_part = pltpu.VMEM((na, half, dim), BF16)
    return pl.pallas_call(
        functools.partial(kernel, n),
        out_shape=jax.ShapeDtypeStruct((half, dim), BF16),
        in_specs=[vmem] * 8,
        out_specs=vmem,
        scratch_shapes=[
            pltpu.VMEM((na, rows, width), BF16),
            pltpu.VMEM((2, count // 2, dim), BF16),
            pltpu.VMEM((2 * heads, count, PAIR), BF16),
            pltpu.VMEM((2 * heads, HEAD_DIM + EXTRA, count), BF16),
            pltpu.VMEM((3,) + w_up.shape, BF16),
            pltpu.VMEM((3,) + w_down.shape, BF16),
            partial, partial, partial,
            stats, stats, stats,
            pltpu.VMEM((width, rows), F32),
            pltpu.VMEM((2, half, width), BF16),
            pltpu.VMEM((half, width), BF16),
            pltpu.VMEM((na, half, dim), BF16),
            mlp_part, mlp_part,
            pltpu.VMEM((half, dim), F32),
            dma((4,)), dma((12,)), dma((2 * na,)), dma((na,)),
            dma((na,)), dma((na,)), dma((na,)), dma((na,)), dma((2,)),
            dma((2 * na,)), dma((na,)), dma((na,)), dma((na,)),
        ],
        compiler_params=pltpu.CompilerParams(
            collective_id=0, has_side_effects=True, vmem_limit_bytes=58 * 1024 * 1024
        ),
        cost_estimate=pl.CostEstimate(
            flops=12_000_000_000, bytes_accessed=9_000_000, transcendentals=17_000_000
        ),
    )(latents, cells, w_query, w_key, w_value, w_out, w_up, w_down)


def solution(mesh):
    return jax.shard_map(
        body,
        mesh=mesh,
        in_specs=(
            P(("group", "cell"), None),
            P(("group", "cell"), None),
            P(None, "head"),
            P(None, "head"),
            P(None, "head"),
            P(),
            P(None, ("cell", "head")),
            P(("cell", "head"), None),
        ),
        out_specs=P(("group", "cell", "head"), None),
        check_vma=False,
    )
```
